32 devices in a mesh: member: 2 (over x), space: 16 (over z, y, core).
Axes of the slice: x: 2, y: 2, z: 4, core: 2. Of those that a mesh axis runs over, the one named last changes fastest.
Arguments:
- state_field: bfloat16 [78, 64, 256], P(None, 'space'), may hold values from -6 to 6
- target_field: bfloat16 [78, 64, 256], P(None, 'space'), may hold values from -6 to 6
- noise_seeds: int32 [4], P('member'), may hold values from 0 to 999999
- first_weight: bfloat16 [9, 128, 86], replicated, may hold values from -0.21875 to 0.21875
- first_bias: float32 [128], replicated, may hold values from -3 to 3
- second_weight: bfloat16 [9, 78, 128], replicated, may hold values from -0.1875 to 0.1875
- second_bias: float32 [78], replicated, may hold values from -2 to 2
Outputs:
- state_gradient: float32 [78, 64, 256], P(None, 'space')
- first_weight_grad: float32 [9, 128, 86], replicated
- first_bias_grad: float32 [128], replicated
- second_weight_grad: float32 [9, 78, 128], replicated
- second_bias_grad: float32 [78], replicated
The draws below stay inside these ranges and needn't reach their ends.
All inputs are finite; a program needn't handle non-finite values.
Results may differ from the reference program's by a relative error of at most 0.0039.
Values may be sent and summed in bfloat16 or wider, within the bound.
A program may use at most 64 MiB of HBM per device.

```python
import math
import jax
import jax.numpy as jnp
from jax import lax

C = 78
HID = 128
LON = 256
NLAT = 64
MEMBERS = 4
CIN = 86


def plant(values, stream_key, least, top_value):
    longest = values.shape.index(max(values.shape))
    spots = []
    for shift in (0, 1):
        where = [jax.random.randint(jax.random.fold_in(stream_key, axis), (), 0, length) for axis, length in enumerate(values.shape)]
        where[longest] = (where[longest] + shift) % values.shape[longest]
        spots.append(tuple(where))
    return values.at[spots[0]].set(least).at[spots[1]].set(top_value)


def levels(own_key, dims, pieces, low, high):
    def one(position, parts):
        draws = jax.random.uniform(jax.random.fold_in(jax.random.fold_in(own_key, 6), position), (parts,), jnp.float32, low / len(pieces), high / len(pieces))
        return jnp.repeat(jnp.exp(draws), dims[position] // parts).reshape((-1,) + (1,) * (len(dims) - position - 1))

    level = one(*pieces[0])
    for cut in pieces[1:]:
        level = level * one(*cut)
    return level


def bell_draw(key, dims, scale, reach, pieces=(), kind=jnp.bfloat16):
    gain = levels(key, dims, pieces, -0.22, 0.18) if pieces else 1.0
    result = jax.random.normal(key, dims, jnp.float32) * scale * gain
    return jnp.minimum(jnp.maximum(result, -reach), reach).astype(kind)


def setup_inputs(seed: int = 0) -> dict:
    seeds = jax.random.split(jax.random.key(seed), 8)
    return {
        "state_field": bell_draw(seeds[0], (C, NLAT, LON), 1.0, 6.0, ((1, 16),)),
        "target_field": bell_draw(seeds[1], (C, NLAT, LON), 1.0, 6.0, ((1, 16),)),
        "noise_seeds": plant(jax.random.randint(seeds[2], (MEMBERS,), 0, 1000000), jax.random.fold_in(seeds[2], 1), 0, 999999).astype(jnp.int32),
        "first_weight": bell_draw(seeds[3], (9, HID, CIN), (9 * CIN) ** -0.5, 0.21875),
        "first_bias": bell_draw(seeds[4], (HID,), 0.5, 3.0, (), jnp.float32),
        "second_weight": bell_draw(seeds[5], (9, C, HID), (9 * HID) ** -0.5, 0.1875),
        "second_bias": bell_draw(seeds[6], (C,), 0.3, 2.0, (), jnp.float32),
    }


SMOOTH_SQ = 0.01
TAP_STEPS = ((-1, -1), (-1, 0), (-1, 1), (0, -1), (0, 0), (0, 1), (1, -1), (1, 0), (1, 1))

def rounded(values):
    return lax.optimization_barrier(values.astype(jnp.bfloat16)).astype(jnp.float32)

def smooth_slope(difference):
    return difference / jnp.sqrt(difference * difference + SMOOTH_SQ)

def silu_slope(pre_act):
    gate_value = jax.nn.sigmoid(pre_act)
    return gate_value * (1.0 + pre_act * (1.0 - gate_value))

def member_noise(seed_value, row_count, lon_count, channels):
    row_ids = jnp.arange(row_count, dtype=jnp.int32)[None, :, None]
    lon_ids = jnp.arange(lon_count, dtype=jnp.int32)[None, None, :]
    chan_ids = jnp.arange(channels, dtype=jnp.int32)[:, None, None]
    hashed = (seed_value * 7 + row_ids * 1439 + lon_ids * 31 + chan_ids * 104729) % 65521
    folded = hashed % 46340
    mixed_hash = (folded * folded + chan_ids * 97 + lon_ids * 13) % 65521
    return mixed_hash.astype(jnp.float32) / 32760.0 - 1.0

def shifted(field, row_step, lon_step):
    padded = jnp.pad(field, ((0, 0), (1, 1), (0, 0)))
    row_band = padded[:, 1 + row_step:1 + row_step + field.shape[1], :]
    return jnp.roll(row_band, -lon_step, axis=2)

def convolve(weight, field):
    running = jnp.zeros((weight.shape[1],) + field.shape[1:], jnp.float32)
    for tap_index, (row_step, lon_step) in enumerate(TAP_STEPS):
        running = running + jnp.einsum('oi,irl->orl', weight[tap_index], shifted(field, row_step, lon_step))
    return running

def transposed(weight, gradient):
    running = jnp.zeros((weight.shape[2],) + gradient.shape[1:], jnp.float32)
    for tap_index, (row_step, lon_step) in enumerate(TAP_STEPS):
        running = running + jnp.einsum('oi,orl->irl', weight[tap_index], shifted(gradient, -row_step, -lon_step))
    return running

def weight_grad(gradient, field):
    tap_terms = []
    for row_step, lon_step in TAP_STEPS:
        tap_terms.append(jnp.einsum('orl,irl->oi', gradient, shifted(field, row_step, lon_step)))
    return jnp.stack(tap_terms, axis=0)

def reference(state_field, target_field, noise_seeds, first_weight, first_bias, second_weight, second_bias):
    members = noise_seeds.shape[0]
    channels, row_count, lon_count = state_field.shape
    noise_count = first_weight.shape[2] - channels
    state_wide = state_field.astype(jnp.float32)
    target_wide = target_field.astype(jnp.float32)
    weight_one = first_weight.astype(jnp.float32)
    weight_two = second_weight.astype(jnp.float32)
    area_weight = jnp.sin(math.pi * (jnp.arange(row_count, dtype=jnp.float32) + 0.5) / row_count)[:, None]

    def forward(seed_value):
        noise_field = rounded(member_noise(seed_value, row_count, lon_count, noise_count))
        inputs = jnp.concatenate([state_wide, noise_field], axis=0)
        pre_act = first_bias[:, None, None] + convolve(weight_one, inputs)
        hidden = rounded(jax.nn.silu(pre_act))
        output_field = (state_wide + second_bias[:, None, None] + convolve(weight_two, hidden)).astype(jnp.bfloat16)
        return (inputs, pre_act, hidden, output_field)
    outputs = lax.map(lambda seed_value: forward(seed_value)[3], noise_seeds)

    def backward(carry, item):
        seed_value, output_field = item
        inputs, pre_act, hidden, unused_output = forward(seed_value)
        own_values = output_field.astype(jnp.float32)

        def add_pair(member_index, running):
            partner = lax.dynamic_index_in_dim(outputs, member_index, 0, keepdims=False).astype(jnp.float32)
            return running + smooth_slope(own_values - partner)
        pair_sum = lax.fori_loop(0, members, add_pair, jnp.zeros(own_values.shape, jnp.float32))
        target_slope = smooth_slope(own_values - target_wide)
        out_grad = rounded(area_weight * (target_slope / members - pair_sum / (members * (members - 1))))
        first_w, first_b, second_w, second_b, state_acc = carry
        second_w = second_w + weight_grad(out_grad, hidden)
        second_b = second_b + lax.optimization_barrier(jnp.sum(out_grad, axis=(1, 2)))
        pre_grad = rounded(transposed(weight_two, out_grad) * silu_slope(pre_act))
        first_b = first_b + lax.optimization_barrier(jnp.sum(pre_grad, axis=(1, 2)))
        first_w = first_w + weight_grad(pre_grad, inputs)
        state_acc = state_acc + out_grad + transposed(weight_one[:, :, :channels], pre_grad)
        return ((first_w, first_b, second_w, second_b, state_acc), None)
    start = (jnp.zeros(first_weight.shape, jnp.float32), jnp.zeros(first_bias.shape, jnp.float32), jnp.zeros(second_weight.shape, jnp.float32), jnp.zeros(second_bias.shape, jnp.float32), jnp.zeros(state_field.shape, jnp.float32))
    finals, unused_stack = lax.scan(backward, start, (noise_seeds, outputs))
    first_w, first_b, second_w, second_b, state_gradient = finals
    squares = jnp.sum(first_w * first_w) + jnp.sum(first_b * first_b) + jnp.sum(second_w * second_w) + jnp.sum(second_b * second_b)
    weight_count = first_w.size + first_b.size + second_w.size + second_b.size
    factor = jnp.minimum(1.0, math.sqrt(weight_count) / jnp.sqrt(squares))
    return (state_gradient, first_w * factor, first_b * factor, second_w * factor, second_b * factor)
```

```python
import functools
import math

import jax
import jax.numpy as jnp
from jax import lax
from jax.experimental import pallas as pl
from jax.experimental.pallas import tpu as pltpu
from jax.sharding import PartitionSpec as P

SMOOTH_SQ = 0.01
MESH = pl.DeviceIdType.MESH
F32 = jnp.float32
BF16 = jnp.bfloat16
NT = (((1,), (1,)), ((), ()))


def modulo(value, divisor):
    quotient = (value.astype(F32) * (1.0 / divisor)).astype(jnp.int32)
    left = value - quotient * divisor
    left = jnp.where(left < 0, left + divisor, left)
    return jnp.where(left >= divisor, left - divisor, left)


def slope(diff):
    return diff * lax.rsqrt(diff * diff + SMOOTH_SQ)


def dot(a, b):
    return jnp.dot(a, b, preferred_element_type=F32)


def dot_nt(a, b):
    return lax.dot_general(a, b, NT, preferred_element_type=F32)


def kernel(
    space_size, cfg,
    fields, seeds, aux, w1s, w1n, b1, w2f, b2, w2t, w1t,
    grads_out, state_out,
    ext, all_seeds, xs3, xn3, pre_common, h3, gate, outs, og3, pg3, total, recv1, send2, recv2, send3, recv3, recv4, part4,
    gathered,
    halo_send, halo_recv, seed_sem, state_sem, red_send, red_recv, gat_send, gat_recv, more_send, more_recv,
):
    C, CP, HID, LON, BAND, MEM, NOISE = cfg
    own = BAND // 2
    s = lax.axis_index("space")
    h = lax.axis_index("member")
    has_left = s > 0
    has_right = s < space_size - 1
    bits = (space_size.bit_length() - 1) - 4
    core = s % 2
    quad = h * 2 + (s // 2) % 2
    quad_y = (s // 2) % 2
    zed = (s // 4) % 4

    def flip(value, mask, unit, width):
        digit = (value // unit) % width
        flipped = jnp.int32(0)
        place = 1
        while place < width:
            bit = (digit // place) % 2
            if mask & place:
                bit = 1 - bit
            flipped = flipped + bit * place
            place *= 2
        return value + (flipped - digit) * unit

    def at(member, space):
        return (member, space)

    core_peer = at(h, flip(s, 1, 1, 2))
    member_peer = at(1 - h, s)
    quad_peers = []
    for d in (1, 2, 3):
        quad_peers.append(at(1 - h if d & 2 else h, flip(s, 1, 2, 2) if d & 1 else s))
    zed_peers = [at(h, flip(s, d, 4, 4)) for d in (1, 2, 3)]
    far_peers = [at(h, flip(s, 1, 16 << k, 2)) for k in range(bits)]

    barrier = pltpu.get_barrier_semaphore()
    fixed = [core_peer, member_peer] + quad_peers + zed_peers + far_peers
    for peer in fixed:
        pl.semaphore_signal(barrier, inc=1, device_id=peer, device_id_type=MESH)

    @pl.when(has_left)
    def _():
        pl.semaphore_signal(barrier, inc=1, device_id=at(h, s - 1), device_id_type=MESH)

    @pl.when(has_right)
    def _():
        pl.semaphore_signal(barrier, inc=1, device_id=at(h, s + 1), device_id_type=MESH)

    pl.semaphore_wait(
        barrier, len(fixed) + has_left.astype(jnp.int32) + has_right.astype(jnp.int32)
    )

    width = BAND * LON
    to_left = pltpu.make_async_remote_copy(
        src_ref=fields, dst_ref=ext.at[:, 2 * width : 3 * width],
        send_sem=halo_send.at[0], recv_sem=halo_recv.at[0],
        device_id=at(h, s - 1), device_id_type=MESH,
    )
    to_right = pltpu.make_async_remote_copy(
        src_ref=fields, dst_ref=ext.at[:, 0:width],
        send_sem=halo_send.at[1], recv_sem=halo_recv.at[1],
        device_id=at(h, s + 1), device_id_type=MESH,
    )
    swap = pltpu.make_async_remote_copy(
        src_ref=seeds, dst_ref=all_seeds.at[h],
        send_sem=seed_sem.at[0], recv_sem=seed_sem.at[1],
        device_id=member_peer, device_id_type=MESH,
    )
    swap.start()

    @pl.when(has_left)
    def _():
        to_left.start()

    @pl.when(has_right)
    def _():
        to_right.start()

    all_seeds[h] = seeds[...]
    ext[:, width : 2 * width] = fields[...]
    total[...] = jnp.zeros_like(total)

    @pl.when(jnp.logical_not(has_left))
    def _():
        ext[:, 0:width] = jnp.zeros((2 * CP, width), BF16)

    @pl.when(jnp.logical_not(has_right))
    def _():
        ext[:, 2 * width : 3 * width] = jnp.zeros((2 * CP, width), BF16)

    swap.wait()

    n_in = 2 * own + 6
    base_row = s * BAND + h * own - 4
    lon = lax.broadcasted_iota(jnp.int32, (NOISE, LON), 1)
    chan = lax.broadcasted_iota(jnp.int32, (NOISE, LON), 0)
    lane_term = lon * 31 + chan * 104729
    late_term = chan * 97 + lon * 13

    def noise_member(m, carry):
        seed = all_seeds[m // 2, pl.ds(m % 2, 1), :]
        seed7 = jnp.concatenate([seed, seed], axis=1) * 7
        for j in range(10):
            hashed = modulo(jnp.maximum(seed7 + (base_row + j) * 1439 + lane_term, 0), 65521)
            folded = jnp.where(hashed >= 46340, hashed - 46340, hashed)
            mixed = modulo(folded * folded + late_term, 65521)
            value = mixed.astype(F32) / 32760.0 - 1.0
            value = value * aux[8 + j : 9 + j, :]
            value = value.astype(BF16).astype(F32)
            zero = jnp.zeros_like(value)
            for b, shift in enumerate((1, 0, LON - 1)):
                moved = pltpu.roll(value, shift, 1) if shift else value
                xn3[m, b * 16 : b * 16 + 16, j * LON : (j + 1) * LON] = jnp.concatenate(
                    [moved, zero], axis=0
                ).astype(BF16)
        return carry

    lax.fori_loop(0, MEM, noise_member, 0)

    @pl.when(has_left)
    def _():
        to_left.wait_send()
        to_right.wait_recv()

    @pl.when(has_right)
    def _():
        to_right.wait_send()
        to_left.wait_recv()

    def ext_cols(j):
        return pl.ds(pl.multiple_of(h * (own * LON), own * LON) + j * LON, LON)

    row_of = lax.broadcasted_iota(jnp.int32, (CP, LON), 0)
    for j in range(10):
        value = ext[0:CP, ext_cols(j)].astype(F32)
        for b, shift in enumerate((1, 0, LON - 1)):
            moved = pltpu.roll(value, shift, 1) if shift else jnp.where(row_of == C, 1.0, value)
            xs3[b * CP : (b + 1) * CP, j * LON : (j + 1) * LON] = moved.astype(BF16)

    def cols(j, n=1):
        return slice(j * LON, (j + n) * LON)

    for k in range(8):
        pre_common[:, cols(k)] = (
            dot(w1s[0], xs3[:, cols(k)])
            + dot(w1s[1], xs3[:, cols(k + 1)])
            + dot(w1s[2], xs3[:, cols(k + 2)])
            + b1[...]
        )

    def forward(m, carry):
        for k in range(8):
            noise9 = jnp.concatenate([xn3[m, :, cols(k + a)] for a in range(3)], axis=0)
            pre = pre_common[:, cols(k)] + dot(w1n[...], noise9)
            sig = 1.0 / (1.0 + jnp.exp(-pre))
            hid = pre * sig * aux[9 + k : 10 + k, :]
            hid = hid.astype(BF16).astype(F32)
            if 2 <= k < 6:
                gate[m, :, cols(k - 2)] = sig * (1.0 + pre * (1.0 - sig)) * aux[9 + k : 10 + k, :]
            for b, shift in enumerate((1, 0, LON - 1)):
                moved = pltpu.roll(hid, shift, 1) if shift else hid
                h3[m, b * HID : (b + 1) * HID, cols(k)] = moved.astype(BF16)
        for n in range(6):
            hid9 = jnp.concatenate([h3[m, :, cols(n + a)] for a in range(3)], axis=0)
            state = ext[0:CP, ext_cols(n + 2)].astype(F32)
            outs[m, :, cols(n)] = (state + b2[...] + dot(w2f[...], hid9)).astype(BF16)
        return carry

    lax.fori_loop(0, MEM, forward, 0)

    for n in range(6):
        values = [outs[m, :, cols(n)].astype(F32) for m in range(MEM)]
        target = ext[CP : 2 * CP, ext_cols(n + 2)].astype(F32)
        sums = [jnp.zeros((CP, LON), F32)] * MEM
        for m in range(MEM):
            for q in range(m + 1, MEM):
                term = slope(values[m] - values[q])
                sums[m] = sums[m] + term
                sums[q] = sums[q] - term
        for m in range(MEM):
            grad = aux[n : n + 1, :] * (
                slope(values[m] - target) * (1.0 / MEM) - sums[m] * (1.0 / (MEM * (MEM - 1)))
            )
            grad = grad.astype(BF16).astype(F32)
            for b, shift in enumerate((LON - 1, 0, 1)):
                moved = pltpu.roll(grad, shift, 1) if shift else grad
                og3[m, b * CP : (b + 1) * CP, cols(n)] = moved.astype(BF16)

    first_row = jnp.where(
        lax.broadcasted_iota(jnp.int32, (8, own * LON), 0) == 0, 1.0, 0.0
    ).astype(BF16)
    per_tap = CP + NOISE
    second = 9 * per_tap
    keep_c = lax.broadcasted_iota(jnp.int32, (CP, HID), 0) < C

    def backward(m, carry):
        for p in range(4):
            hidden_grad = (
                dot(w2t[0], og3[m, :, cols(p + 2)])
                + dot(w2t[1], og3[m, :, cols(p + 1)])
                + dot(w2t[2], og3[m, :, cols(p)])
            )
            grad = (hidden_grad * gate[m, :, cols(p)]).astype(BF16).astype(F32)
            for b, shift in enumerate((LON - 1, 0, 1)):
                moved = pltpu.roll(grad, shift, 1) if shift else grad
                pg3[m, b * HID : (b + 1) * HID, cols(p)] = moved.astype(BF16)
        own_out = og3[m, CP : 2 * CP, cols(2, own)]
        own_pre = pg3[m, HID : 2 * HID, cols(1, own)]
        for a in range(3):
            part = dot_nt(own_out, h3[m, :, cols(2 + a, own)])
            first_s = dot_nt(xs3[:, cols(3 + a, own)], own_pre)
            first_n = dot_nt(xn3[m, :, cols(3 + a, own)], own_pre)
            for b in range(3):
                tap = 3 * a + b
                at_row = second + tap * CP
                total[at_row : at_row + CP, :] += part[:, b * HID : (b + 1) * HID]
                chunk = first_s[b * CP : (b + 1) * CP]
                if tap != 4:
                    chunk = jnp.where(keep_c, chunk, 0.0)
                total[tap * per_tap : tap * per_tap + CP, :] += chunk
                total[tap * per_tap + CP : (tap + 1) * per_tap, :] += first_n[
                    b * 16 : b * 16 + NOISE
                ]
        at_row = second + 9 * CP
        total[at_row : at_row + 8, 0:CP] += dot_nt(first_row, own_out)
        return carry

    lax.fori_loop(0, MEM, backward, 0)

    rows = total.shape[0]
    half, quarter, piece = rows // 2, rows // 8, rows // 32
    keep1 = pl.multiple_of(core * half, half)
    away1 = pl.multiple_of((1 - core) * half, half)
    first_copy = pltpu.make_async_remote_copy(
        src_ref=total.at[pl.ds(away1, half)], dst_ref=recv1,
        send_sem=red_send.at[0], recv_sem=red_recv.at[0],
        device_id=core_peer, device_id_type=MESH,
    )
    first_copy.start()

    for t in range(own):
        value = jnp.zeros((CP, LON), F32)
        for m in range(MEM):
            grad9 = jnp.concatenate([pg3[m, :, cols(t + 2 - a)] for a in range(3)], axis=0)
            value = value + dot(w1t[...], grad9)
            value = value + og3[m, CP : 2 * CP, cols(t + 2)].astype(F32)
        state_out[h, :, cols(t)] = value
    state_copy = pltpu.make_async_remote_copy(
        src_ref=state_out.at[h], dst_ref=state_out.at[h],
        send_sem=state_sem.at[0], recv_sem=state_sem.at[1],
        device_id=member_peer, device_id_type=MESH,
    )

    first_copy.wait()
    total[pl.ds(keep1, half), :] += recv1[...]
    send2[...] = total[pl.ds(keep1, half), :].astype(BF16)
    copies = []
    for d in (1, 2, 3):
        qm = 1 - h if d & 2 else h
        qy = 1 - quad_y if d & 1 else quad_y
        start = pl.multiple_of((qm * 2 + qy) * quarter, quarter)
        copies.append(pltpu.make_async_remote_copy(
            src_ref=send2.at[pl.ds(start, quarter)], dst_ref=recv2.at[d - 1],
            send_sem=red_send.at[d], recv_sem=red_recv.at[d],
            device_id=quad_peers[d - 1], device_id_type=MESH,
        ))
        copies[-1].start()
    state_copy.start()
    for copy in copies:
        copy.wait()
    keep2 = pl.multiple_of(keep1 + quad * quarter, quarter)
    value = total[pl.ds(keep2, quarter), :]
    for d in range(3):
        value = value + recv2[d].astype(F32)
    total[pl.ds(keep2, quarter), :] = value
    send3[...] = value.astype(BF16)
    copies = []
    for d in (1, 2, 3):
        other = flip(zed, d, 1, 4)
        start = pl.multiple_of(other * piece, piece)
        copies.append(pltpu.make_async_remote_copy(
            src_ref=send3.at[pl.ds(start, piece)], dst_ref=recv3.at[d - 1],
            send_sem=red_send.at[3 + d], recv_sem=red_recv.at[3 + d],
            device_id=zed_peers[d - 1], device_id_type=MESH,
        ))
        copies[-1].start()
    for copy in copies:
        copy.wait()
    keep3 = pl.multiple_of(keep2 + zed * piece, piece)
    value = total[pl.ds(keep3, piece), :]
    for d in range(3):
        value = value + recv3[d].astype(F32)
    for k in range(bits):
        part4[k] = value
        copy = pltpu.make_async_remote_copy(
            src_ref=part4.at[k], dst_ref=recv4.at[k],
            send_sem=more_send.at[k], recv_sem=more_recv.at[k],
            device_id=far_peers[k], device_id_type=MESH,
        )
        copy.start()
        copy.wait()
        value = value + recv4[k]
    gathered[pl.ds(keep3, piece), :] = value.astype(BF16)

    slot = 0
    for start, size, peers in (
        (keep3, piece, zed_peers), (keep2, quarter, quad_peers), (keep1, half, [core_peer])
    ):
        copies = []
        for peer in peers:
            copies.append(pltpu.make_async_remote_copy(
                src_ref=gathered.at[pl.ds(start, size)], dst_ref=gathered.at[pl.ds(start, size)],
                send_sem=gat_send.at[slot], recv_sem=gat_recv.at[slot],
                device_id=peer, device_id_type=MESH,
            ))
            copies[-1].start()
            slot += 1
        for copy in copies:
            copy.wait()

    everything = gathered[...].astype(F32)
    squares = jnp.sum(everything * everything)
    count = 9 * HID * (C + NOISE) + HID + 9 * C * HID + C
    norm = jnp.sqrt(jnp.broadcast_to(squares, (8, HID)))
    factor = jnp.minimum(1.0, math.sqrt(count) / norm)
    grads_out[...] = everything * factor[0:1, :]
    state_copy.wait()


def local(
    state_field, target_field, noise_seeds, first_weight, first_bias, second_weight, second_bias
):
    C, band, lon = state_field.shape
    hid = first_weight.shape[1]
    noise = first_weight.shape[2] - C
    space_size = lax.axis_size("space")
    members = noise_seeds.shape[0] * lax.axis_size("member")
    total_rows = band * space_size
    cp = (C + 1 + 15) // 16 * 16
    own = band // 2
    fields = jnp.pad(
        jnp.stack([state_field, target_field]), ((0, 0), (0, cp - C), (0, 0), (0, 0))
    ).reshape(2 * cp, band * lon)
    seeds = jnp.broadcast_to(
        jnp.pad(noise_seeds, (0, 8 - noise_seeds.shape[0]))[:, None], (8, 128)
    )
    base = lax.axis_index("space") * band + lax.axis_index("member") * own
    row_ids = base - 4 + jnp.arange(10, dtype=jnp.int32)
    inside = ((row_ids >= 0) & (row_ids < total_rows)).astype(F32)
    out_ids = row_ids[2:8]
    area = jnp.sin(math.pi * (out_ids.astype(F32) + 0.5) / total_rows) * inside[2:8]
    aux = jnp.concatenate([area, jnp.zeros((2,), F32), inside, jnp.zeros((6,), F32)])
    aux = jnp.broadcast_to(aux[:, None], (24, lon))
    w1_state = jnp.pad(first_weight[:, :, :C], ((0, 0), (0, 0), (0, cp - C)))
    w1_noise = jnp.pad(first_weight[:, :, C:], ((0, 0), (0, 0), (0, 16 - noise)))
    w2 = jnp.pad(second_weight, ((0, 0), (0, cp - C), (0, 0)))
    w1s = w1_state.reshape(3, 3, hid, cp).transpose(0, 2, 1, 3).reshape(3, hid, 3 * cp)
    w1n = w1_noise.transpose(1, 0, 2).reshape(hid, 9 * 16)
    w2f = w2.transpose(1, 0, 2).reshape(cp, 9 * hid)
    w2t = w2.reshape(3, 3, cp, hid).transpose(0, 3, 1, 2).reshape(3, hid, 3 * cp)
    w1t = w1_state.transpose(2, 0, 1).reshape(cp, 9 * hid)
    b1 = first_bias[:, None]
    b2 = jnp.pad(second_bias, (0, cp - C))[:, None]
    per_tap = cp + noise
    used = 9 * per_tap + 9 * cp + 8
    rows = (used + 511) // 512 * 512
    half, quarter, piece = rows // 2, rows // 8, rows // 32
    far = max(1, space_size.bit_length() - 5)
    vmem = pl.BlockSpec(memory_space=pltpu.VMEM)
    dma = pltpu.SemaphoreType.DMA
    cfg = (C, cp, hid, lon, band, members, noise)
    grads, state = pl.pallas_call(
        functools.partial(kernel, space_size, cfg),
        out_shape=(
            jax.ShapeDtypeStruct((rows, hid), F32),
            jax.ShapeDtypeStruct((2, cp, own * lon), F32),
        ),
        in_specs=[vmem] * 10,
        out_specs=(vmem, vmem),
        scratch_shapes=[
            pltpu.VMEM((2 * cp, 3 * band * lon), BF16),
            pltpu.VMEM((2, 8, 128), jnp.int32),
            pltpu.VMEM((3 * cp, 10 * lon), BF16),
            pltpu.VMEM((members, 48, 10 * lon), BF16),
            pltpu.VMEM((hid, 8 * lon), F32),
            pltpu.VMEM((members, 3 * hid, 8 * lon), BF16),
            pltpu.VMEM((members, hid, 4 * lon), F32),
            pltpu.VMEM((members, cp, 6 * lon), BF16),
            pltpu.VMEM((members, 3 * cp, 6 * lon), BF16),
            pltpu.VMEM((members, 3 * hid, 4 * lon), BF16),
            pltpu.VMEM((rows, hid), F32),
            pltpu.VMEM((half, hid), F32),
            pltpu.VMEM((half, hid), BF16),
            pltpu.VMEM((3, quarter, hid), BF16),
            pltpu.VMEM((quarter, hid), BF16),
            pltpu.VMEM((3, piece, hid), BF16),
            pltpu.VMEM((far, piece, hid), F32),
            pltpu.VMEM((far, piece, hid), F32),
            pltpu.VMEM((rows, hid), BF16),
            dma((2,)), dma((2,)), dma((2,)), dma((2,)),
            dma((7,)), dma((7,)), dma((7,)), dma((7,)), dma((far,)), dma((far,)),
        ],
        compiler_params=pltpu.CompilerParams(
            collective_id=0, has_side_effects=True, vmem_limit_bytes=48 * 1024 * 1024
        ),
    )(fields, seeds, aux, w1s, w1n, b1, w2f, b2, w2t, w1t)
    state_gradient = state.reshape(2, cp, own, lon)[:, :C].transpose(1, 0, 2, 3).reshape(
        C, band, lon
    )
    first = grads[: 9 * per_tap].reshape(9, per_tap, hid)
    first_w = jnp.concatenate([first[:, :C], first[:, cp:]], axis=1).transpose(0, 2, 1)
    first_b = first[4, C]
    second = grads[9 * per_tap : 9 * per_tap + 9 * cp].reshape(9, cp, hid)[:, :C]
    second_b = grads[9 * per_tap + 9 * cp, :C]
    return state_gradient, first_w, first_b, second, second_b


def solution(mesh):
    placed = (P(None, "space", None), P(None, "space", None), P("member"), P(), P(), P(), P())
    return jax.shard_map(
        local,
        mesh=mesh,
        in_specs=placed,
        out_specs=(P(None, "space", None), P(), P(), P(), P()),
        check_vma=False,
    )
```

```python
import functools
import math

import jax
import jax.numpy as jnp
from jax import lax
from jax.experimental import pallas as pl
from jax.experimental.pallas import tpu as pltpu
from jax.sharding import PartitionSpec as P

SMOOTH_SQ = 0.01
MESH = pl.DeviceIdType.MESH
F32 = jnp.float32
BF16 = jnp.bfloat16
NT = (((1,), (1,)), ((), ()))


def modulo(value, divisor):
    quotient = (value.astype(F32) * (1.0 / divisor)).astype(jnp.int32)
    left = value - quotient * divisor
    left = jnp.where(left < 0, left + divisor, left)
    return jnp.where(left >= divisor, left - divisor, left)


def slope(diff):
    return diff * lax.rsqrt(diff * diff + SMOOTH_SQ)


def dot(a, b):
    return jnp.dot(a, b, preferred_element_type=F32)


def dot_nt(a, b):
    return lax.dot_general(a, b, NT, preferred_element_type=F32)


def kernel(
    space_size, cfg,
    fields, seeds, aux, w1s, w1n, b1, w2f, b2, w2t, w1t,
    grads_out, state_out,
    ext, all_seeds, xs3, xn3, pre_common, h3, gate, outs, og3, pg3, total, recv1, send2, recv2, send3, recv3, recv4, part4,
    gathered,
    halo_send, halo_recv, seed_sem, state_sem, red_send, red_recv, gat_send, gat_recv, more_send, more_recv,
):
    C, CP, HID, LON, BAND, MEM, NOISE = cfg
    own = BAND // 2
    s = lax.axis_index("space")
    h = lax.axis_index("member")
    has_left = s > 0
    has_right = s < space_size - 1
    bits = (space_size.bit_length() - 1) - 4
    core = s % 2
    quad = h * 2 + (s // 2) % 2
    quad_y = (s // 2) % 2
    zed = (s // 4) % 4

    def flip(value, mask, unit, width):
        digit = (value // unit) % width
        flipped = jnp.int32(0)
        place = 1
        while place < width:
            bit = (digit // place) % 2
            if mask & place:
                bit = 1 - bit
            flipped = flipped + bit * place
            place *= 2
        return value + (flipped - digit) * unit

    def at(member, space):
        return (member, space)

    core_peer = at(h, flip(s, 1, 1, 2))
    member_peer = at(1 - h, s)
    quad_peers = []
    for d in (1, 2, 3):
        quad_peers.append(at(1 - h if d & 2 else h, flip(s, 1, 2, 2) if d & 1 else s))
    zed_peers = [at(h, flip(s, d, 4, 4)) for d in (1, 2, 3)]
    far_peers = [at(h, flip(s, 1, 16 << k, 2)) for k in range(bits)]

    barrier = pltpu.get_barrier_semaphore()
    fixed = [core_peer, member_peer] + quad_peers + zed_peers + far_peers
    for peer in fixed:
        pl.semaphore_signal(barrier, inc=1, device_id=peer, device_id_type=MESH)

    @pl.when(has_left)
    def _():
        pl.semaphore_signal(barrier, inc=1, device_id=at(h, s - 1), device_id_type=MESH)

    @pl.when(has_right)
    def _():
        pl.semaphore_signal(barrier, inc=1, device_id=at(h, s + 1), device_id_type=MESH)

    all_seeds[h] = seeds[...]
    n_in = 2 * own + 6
    base_row = s * BAND + h * own - 4
    lon = lax.broadcasted_iota(jnp.int32, (NOISE, LON), 1)
    chan = lax.broadcasted_iota(jnp.int32, (NOISE, LON), 0)
    lane_term = lon * 31 + chan * 104729
    late_term = chan * 97 + lon * 13

    def noise_member(m, carry):
        seed = all_seeds[m // 2, pl.ds(m % 2, 1), :]
        seed7 = jnp.concatenate([seed, seed], axis=1) * 7
        for j in range(10):
            hashed = modulo(jnp.maximum(seed7 + (base_row + j) * 1439 + lane_term, 0), 65521)
            folded = jnp.where(hashed >= 46340, hashed - 46340, hashed)
            mixed = modulo(folded * folded + late_term, 65521)
            value = mixed.astype(F32) / 32760.0 - 1.0
            value = value * aux[8 + j : 9 + j, :]
            value = value.astype(BF16).astype(F32)
            zero = jnp.zeros_like(value)
            for b, shift in enumerate((1, 0, LON - 1)):
                moved = pltpu.roll(value, shift, 1) if shift else value
                xn3[m, b * 16 : b * 16 + 16, j * LON : (j + 1) * LON] = jnp.concatenate(
                    [moved, zero], axis=0
                ).astype(BF16)
        return carry

    each = MEM // 2
    lax.fori_loop(h * each, h * each + each, noise_member, 0)
    pl.semaphore_wait(
        barrier, len(fixed) + has_left.astype(jnp.int32) + has_right.astype(jnp.int32)
    )

    width = BAND * LON
    to_left = pltpu.make_async_remote_copy(
        src_ref=fields, dst_ref=ext.at[:, 2 * width : 3 * width],
        send_sem=halo_send.at[0], recv_sem=halo_recv.at[0],
        device_id=at(h, s - 1), device_id_type=MESH,
    )
    to_right = pltpu.make_async_remote_copy(
        src_ref=fields, dst_ref=ext.at[:, 0:width],
        send_sem=halo_send.at[1], recv_sem=halo_recv.at[1],
        device_id=at(h, s + 1), device_id_type=MESH,
    )
    swap = pltpu.make_async_remote_copy(
        src_ref=seeds, dst_ref=all_seeds.at[h],
        send_sem=seed_sem.at[0], recv_sem=seed_sem.at[1],
        device_id=member_peer, device_id_type=MESH,
    )
    swap.start()

    @pl.when(has_left)
    def _():
        to_left.start()

    @pl.when(has_right)
    def _():
        to_right.start()

    ext[:, width : 2 * width] = fields[...]
    total[...] = jnp.zeros_like(total)

    @pl.when(jnp.logical_not(has_left))
    def _():
        ext[:, 0:width] = jnp.zeros((2 * CP, width), BF16)

    @pl.when(jnp.logical_not(has_right))
    def _():
        ext[:, 2 * width : 3 * width] = jnp.zeros((2 * CP, width), BF16)

    swap.wait()
    lax.fori_loop((1 - h) * each, (1 - h) * each + each, noise_member, 0)

    @pl.when(has_left)
    def _():
        to_left.wait_send()
        to_right.wait_recv()

    @pl.when(has_right)
    def _():
        to_right.wait_send()
        to_left.wait_recv()

    def ext_cols(j):
        return pl.ds(pl.multiple_of(h * (own * LON), own * LON) + j * LON, LON)

    row_of = lax.broadcasted_iota(jnp.int32, (CP, LON), 0)
    for j in range(10):
        value = ext[0:CP, ext_cols(j)].astype(F32)
        for b, shift in enumerate((1, 0, LON - 1)):
            moved = pltpu.roll(value, shift, 1) if shift else jnp.where(row_of == C, 1.0, value)
            xs3[b * CP : (b + 1) * CP, j * LON : (j + 1) * LON] = moved.astype(BF16)

    def cols(j, n=1):
        return slice(j * LON, (j + n) * LON)

    for k in range(8):
        pre_common[:, cols(k)] = (
            dot(w1s[0], xs3[:, cols(k)])
            + dot(w1s[1], xs3[:, cols(k + 1)])
            + dot(w1s[2], xs3[:, cols(k + 2)])
            + b1[...]
        )

    def forward(m, carry):
        for k in range(8):
            noise9 = jnp.concatenate([xn3[m, :, cols(k + a)] for a in range(3)], axis=0)
            pre = pre_common[:, cols(k)] + dot(w1n[...], noise9)
            sig = 1.0 / (1.0 + jnp.exp(-pre))
            hid = pre * sig * aux[9 + k : 10 + k, :]
            hid = hid.astype(BF16).astype(F32)
            if 2 <= k < 6:
                gate[m, :, cols(k - 2)] = sig * (1.0 + pre * (1.0 - sig)) * aux[9 + k : 10 + k, :]
            for b, shift in enumerate((1, 0, LON - 1)):
                moved = pltpu.roll(hid, shift, 1) if shift else hid
                h3[m, b * HID : (b + 1) * HID, cols(k)] = moved.astype(BF16)
        for n in range(6):
            hid9 = jnp.concatenate([h3[m, :, cols(n + a)] for a in range(3)], axis=0)
            state = ext[0:CP, ext_cols(n + 2)].astype(F32)
            outs[m, :, cols(n)] = (state + b2[...] + dot(w2f[...], hid9)).astype(BF16)
        return carry

    lax.fori_loop(0, MEM, forward, 0)

    for n in range(6):
        values = [outs[m, :, cols(n)].astype(F32) for m in range(MEM)]
        target = ext[CP : 2 * CP, ext_cols(n + 2)].astype(F32)
        sums = [jnp.zeros((CP, LON), F32)] * MEM
        for m in range(MEM):
            for q in range(m + 1, MEM):
                term = slope(values[m] - values[q])
                sums[m] = sums[m] + term
                sums[q] = sums[q] - term
        for m in range(MEM):
            grad = aux[n : n + 1, :] * (
                slope(values[m] - target) * (1.0 / MEM) - sums[m] * (1.0 / (MEM * (MEM - 1)))
            )
            grad = grad.astype(BF16).astype(F32)
            for b, shift in enumerate((LON - 1, 0, 1)):
                moved = pltpu.roll(grad, shift, 1) if shift else grad
                og3[m, b * CP : (b + 1) * CP, cols(n)] = moved.astype(BF16)

    first_row = jnp.where(
        lax.broadcasted_iota(jnp.int32, (8, own * LON), 0) == 0, 1.0, 0.0
    ).astype(BF16)
    per_tap = CP + NOISE
    second = 9 * per_tap
    keep_c = lax.broadcasted_iota(jnp.int32, (CP, HID), 0) < C

    def backward(m, carry):
        for p in range(4):
            hidden_grad = (
                dot(w2t[0], og3[m, :, cols(p + 2)])
                + dot(w2t[1], og3[m, :, cols(p + 1)])
                + dot(w2t[2], og3[m, :, cols(p)])
            )
            grad = (hidden_grad * gate[m, :, cols(p)]).astype(BF16).astype(F32)
            for b, shift in enumerate((LON - 1, 0, 1)):
                moved = pltpu.roll(grad, shift, 1) if shift else grad
                pg3[m, b * HID : (b + 1) * HID, cols(p)] = moved.astype(BF16)
        return carry

    lax.fori_loop(0, MEM, backward, 0)

    for t in range(own):
        value = jnp.zeros((CP, LON), F32)
        for m in range(MEM):
            grad9 = jnp.concatenate([pg3[m, :, cols(t + 2 - a)] for a in range(3)], axis=0)
            value = value + dot(w1t[...], grad9)
            value = value + og3[m, CP : 2 * CP, cols(t + 2)].astype(F32)
        state_out[h, :, cols(t)] = value
    state_copy = pltpu.make_async_remote_copy(
        src_ref=state_out.at[h], dst_ref=state_out.at[h],
        send_sem=state_sem.at[0], recv_sem=state_sem.at[1],
        device_id=member_peer, device_id_type=MESH,
    )

    state_copy.start()

    def weights(m, carry):
        own_out = og3[m, CP : 2 * CP, cols(2, own)]
        own_pre = pg3[m, HID : 2 * HID, cols(1, own)]
        for a in range(3):
            part = dot_nt(own_out, h3[m, :, cols(2 + a, own)])
            first_s = dot_nt(xs3[:, cols(3 + a, own)], own_pre)
            first_n = dot_nt(xn3[m, :, cols(3 + a, own)], own_pre)
            for b in range(3):
                tap = 3 * a + b
                at_row = second + tap * CP
                total[at_row : at_row + CP, :] += part[:, b * HID : (b + 1) * HID]
                chunk = first_s[b * CP : (b + 1) * CP]
                if tap != 4:
                    chunk = jnp.where(keep_c, chunk, 0.0)
                total[tap * per_tap : tap * per_tap + CP, :] += chunk
                total[tap * per_tap + CP : (tap + 1) * per_tap, :] += first_n[
                    b * 16 : b * 16 + NOISE
                ]
        at_row = second + 9 * CP
        total[at_row : at_row + 8, 0:CP] += dot_nt(first_row, own_out)
        return carry

    lax.fori_loop(0, MEM, weights, 0)

    rows = total.shape[0]
    half, quarter, piece = rows // 2, rows // 8, rows // 32
    keep1 = pl.multiple_of(core * half, half)
    away1 = pl.multiple_of((1 - core) * half, half)
    first_copy = pltpu.make_async_remote_copy(
        src_ref=total.at[pl.ds(away1, half)], dst_ref=recv1,
        send_sem=red_send.at[0], recv_sem=red_recv.at[0],
        device_id=core_peer, device_id_type=MESH,
    )
    first_copy.start()

    first_copy.wait()
    total[pl.ds(keep1, half), :] += recv1[...]
    send2[...] = total[pl.ds(keep1, half), :].astype(BF16)
    copies = []
    for d in (1, 2, 3):
        qm = 1 - h if d & 2 else h
        qy = 1 - quad_y if d & 1 else quad_y
        start = pl.multiple_of((qm * 2 + qy) * quarter, quarter)
        copies.append(pltpu.make_async_remote_copy(
            src_ref=send2.at[pl.ds(start, quarter)], dst_ref=recv2.at[d - 1],
            send_sem=red_send.at[d], recv_sem=red_recv.at[d],
            device_id=quad_peers[d - 1], device_id_type=MESH,
        ))
        copies[-1].start()
    for copy in copies:
        copy.wait()
    keep2 = pl.multiple_of(keep1 + quad * quarter, quarter)
    value = total[pl.ds(keep2, quarter), :]
    for d in range(3):
        value = value + recv2[d].astype(F32)
    total[pl.ds(keep2, quarter), :] = value
    send3[...] = value.astype(BF16)
    copies = []
    for d in (1, 2, 3):
        other = flip(zed, d, 1, 4)
        start = pl.multiple_of(other * piece, piece)
        copies.append(pltpu.make_async_remote_copy(
            src_ref=send3.at[pl.ds(start, piece)], dst_ref=recv3.at[d - 1],
            send_sem=red_send.at[3 + d], recv_sem=red_recv.at[3 + d],
            device_id=zed_peers[d - 1], device_id_type=MESH,
        ))
        copies[-1].start()
    for copy in copies:
        copy.wait()
    keep3 = pl.multiple_of(keep2 + zed * piece, piece)
    value = total[pl.ds(keep3, piece), :]
    for d in range(3):
        value = value + recv3[d].astype(F32)
    for k in range(bits):
        part4[k] = value
        copy = pltpu.make_async_remote_copy(
            src_ref=part4.at[k], dst_ref=recv4.at[k],
            send_sem=more_send.at[k], recv_sem=more_recv.at[k],
            device_id=far_peers[k], device_id_type=MESH,
        )
        copy.start()
        copy.wait()
        value = value + recv4[k]
    gathered[pl.ds(keep3, piece), :] = value.astype(BF16)

    slot = 0
    for start, size, peers in (
        (keep3, piece, zed_peers), (keep2, quarter, quad_peers), (keep1, half, [core_peer])
    ):
        copies = []
        for peer in peers:
            copies.append(pltpu.make_async_remote_copy(
                src_ref=gathered.at[pl.ds(start, size)], dst_ref=gathered.at[pl.ds(start, size)],
                send_sem=gat_send.at[slot], recv_sem=gat_recv.at[slot],
                device_id=peer, device_id_type=MESH,
            ))
            copies[-1].start()
            slot += 1
        for copy in copies:
            copy.wait()

    everything = gathered[...].astype(F32)
    squares = jnp.sum(everything * everything)
    count = 9 * HID * (C + NOISE) + HID + 9 * C * HID + C
    norm = jnp.sqrt(jnp.broadcast_to(squares, (8, HID)))
    factor = jnp.minimum(1.0, math.sqrt(count) / norm)
    grads_out[...] = everything * factor[0:1, :]
    state_copy.wait()


def local(
    state_field, target_field, noise_seeds, first_weight, first_bias, second_weight, second_bias
):
    C, band, lon = state_field.shape
    hid = first_weight.shape[1]
    noise = first_weight.shape[2] - C
    space_size = lax.axis_size("space")
    members = noise_seeds.shape[0] * lax.axis_size("member")
    total_rows = band * space_size
    cp = (C + 1 + 15) // 16 * 16
    own = band // 2
    fields = jnp.pad(
        jnp.stack([state_field, target_field]), ((0, 0), (0, cp - C), (0, 0), (0, 0))
    ).reshape(2 * cp, band * lon)
    seeds = jnp.broadcast_to(
        jnp.pad(noise_seeds, (0, 8 - noise_seeds.shape[0]))[:, None], (8, 128)
    )
    base = lax.axis_index("space") * band + lax.axis_index("member") * own
    row_ids = base - 4 + jnp.arange(10, dtype=jnp.int32)
    inside = ((row_ids >= 0) & (row_ids < total_rows)).astype(F32)
    out_ids = row_ids[2:8]
    area = jnp.sin(math.pi * (out_ids.astype(F32) + 0.5) / total_rows) * inside[2:8]
    aux = jnp.concatenate([area, jnp.zeros((2,), F32), inside, jnp.zeros((6,), F32)])
    aux = jnp.broadcast_to(aux[:, None], (24, lon))
    w1_state = jnp.pad(first_weight[:, :, :C], ((0, 0), (0, 0), (0, cp - C)))
    w1_noise = jnp.pad(first_weight[:, :, C:], ((0, 0), (0, 0), (0, 16 - noise)))
    w2 = jnp.pad(second_weight, ((0, 0), (0, cp - C), (0, 0)))
    w1s = w1_state.reshape(3, 3, hid, cp).transpose(0, 2, 1, 3).reshape(3, hid, 3 * cp)
    w1n = w1_noise.transpose(1, 0, 2).reshape(hid, 9 * 16)
    w2f = w2.transpose(1, 0, 2).reshape(cp, 9 * hid)
    w2t = w2.reshape(3, 3, cp, hid).transpose(0, 3, 1, 2).reshape(3, hid, 3 * cp)
    w1t = w1_state.transpose(2, 0, 1).reshape(cp, 9 * hid)
    b1 = first_bias[:, None]
    b2 = jnp.pad(second_bias, (0, cp - C))[:, None]
    per_tap = cp + noise
    used = 9 * per_tap + 9 * cp + 8
    rows = (used + 511) // 512 * 512
    half, quarter, piece = rows // 2, rows // 8, rows // 32
    far = max(1, space_size.bit_length() - 5)
    vmem = pl.BlockSpec(memory_space=pltpu.VMEM)
    dma = pltpu.SemaphoreType.DMA
    cfg = (C, cp, hid, lon, band, members, noise)
    grads, state = pl.pallas_call(
        functools.partial(kernel, space_size, cfg),
        out_shape=(
            jax.ShapeDtypeStruct((rows, hid), F32),
            jax.ShapeDtypeStruct((2, cp, own * lon), F32),
        ),
        in_specs=[vmem] * 10,
        out_specs=(vmem, vmem),
        scratch_shapes=[
            pltpu.VMEM((2 * cp, 3 * band * lon), BF16),
            pltpu.VMEM((2, 8, 128), jnp.int32),
            pltpu.VMEM((3 * cp, 10 * lon), BF16),
            pltpu.VMEM((members, 48, 10 * lon), BF16),
            pltpu.VMEM((hid, 8 * lon), F32),
            pltpu.VMEM((members, 3 * hid, 8 * lon), BF16),
            pltpu.VMEM((members, hid, 4 * lon), F32),
            pltpu.VMEM((members, cp, 6 * lon), BF16),
            pltpu.VMEM((members, 3 * cp, 6 * lon), BF16),
            pltpu.VMEM((members, 3 * hid, 4 * lon), BF16),
            pltpu.VMEM((rows, hid), F32),
            pltpu.VMEM((half, hid), F32),
            pltpu.VMEM((half, hid), BF16),
            pltpu.VMEM((3, quarter, hid), BF16),
            pltpu.VMEM((quarter, hid), BF16),
            pltpu.VMEM((3, piece, hid), BF16),
            pltpu.VMEM((far, piece, hid), F32),
            pltpu.VMEM((far, piece, hid), F32),
            pltpu.VMEM((rows, hid), BF16),
            dma((2,)), dma((2,)), dma((2,)), dma((2,)),
            dma((7,)), dma((7,)), dma((7,)), dma((7,)), dma((far,)), dma((far,)),
        ],
        compiler_params=pltpu.CompilerParams(
            collective_id=0, has_side_effects=True, vmem_limit_bytes=48 * 1024 * 1024
        ),
    )(fields, seeds, aux, w1s, w1n, b1, w2f, b2, w2t, w1t)
    state_gradient = state.reshape(2, cp, own, lon)[:, :C].transpose(1, 0, 2, 3).reshape(
        C, band, lon
    )
    first = grads[: 9 * per_tap].reshape(9, per_tap, hid)
    first_w = jnp.concatenate([first[:, :C], first[:, cp:]], axis=1).transpose(0, 2, 1)
    first_b = first[4, C]
    second = grads[9 * per_tap : 9 * per_tap + 9 * cp].reshape(9, cp, hid)[:, :C]
    second_b = grads[9 * per_tap + 9 * cp, :C]
    return state_gradient, first_w, first_b, second, second_b


def solution(mesh):
    placed = (P(None, "space", None), P(None, "space", None), P("member"), P(), P(), P(), P())
    return jax.shard_map(
        local,
        mesh=mesh,
        in_specs=placed,
        out_specs=(P(None, "space", None), P(), P(), P(), P()),
        check_vma=False,
    )
```

```python
import functools
import math

import jax
import jax.numpy as jnp
from jax import lax
from jax.experimental import pallas as pl
from jax.experimental.pallas import tpu as pltpu
from jax.sharding import PartitionSpec as P

SMOOTH_SQ = 0.01
MESH = pl.DeviceIdType.MESH
F32 = jnp.float32
BF16 = jnp.bfloat16
NT = (((1,), (1,)), ((), ()))


def modulo(value, divisor):
    quotient = (value.astype(F32) * (1.0 / divisor)).astype(jnp.int32)
    left = value - quotient * divisor
    left = jnp.where(left < 0, left + divisor, left)
    return jnp.where(left >= divisor, left - divisor, left)


def slope(diff):
    return diff * lax.rsqrt(diff * diff + SMOOTH_SQ)


def dot(a, b):
    return jnp.dot(a, b, preferred_element_type=F32)


def dot_nt(a, b):
    return lax.dot_general(a, b, NT, preferred_element_type=F32)


def kernel(
    space_size, cfg,
    fields, seeds, aux, w1s, w1n, b1, w2f, b2, w2t, w1t,
    grads_out, state_out,
    ext, all_seeds, xs3, xn3, pre_common, h3, gate, outs, og3, pg3, total, recv1, send2, recv2, send3, recv3, recv4, part4,
    gathered,
    halo_send, halo_recv, seed_sem, state_sem, red_send, red_recv, gat_send, gat_recv, more_send, more_recv,
):
    C, CP, HID, LON, BAND, MEM, NOISE = cfg
    own = BAND // 2
    s = lax.axis_index("space")
    h = lax.axis_index("member")
    has_left = s > 0
    has_right = s < space_size - 1
    bits = (space_size.bit_length() - 1) - 4
    core = s % 2
    quad = h * 2 + (s // 2) % 2
    quad_y = (s // 2) % 2
    zed = (s // 4) % 4

    def flip(value, mask, unit, width):
        digit = (value // unit) % width
        flipped = jnp.int32(0)
        place = 1
        while place < width:
            bit = (digit // place) % 2
            if mask & place:
                bit = 1 - bit
            flipped = flipped + bit * place
            place *= 2
        return value + (flipped - digit) * unit

    def at(member, space):
        return (member, space)

    core_peer = at(h, flip(s, 1, 1, 2))
    member_peer = at(1 - h, s)
    quad_peers = []
    for d in (1, 2, 3):
        quad_peers.append(at(1 - h if d & 2 else h, flip(s, 1, 2, 2) if d & 1 else s))
    zed_peers = [at(h, flip(s, d, 4, 4)) for d in (1, 2, 3)]
    far_peers = [at(h, flip(s, 1, 16 << k, 2)) for k in range(bits)]

    barrier = pltpu.get_barrier_semaphore()
    fixed = [core_peer, member_peer] + quad_peers + zed_peers + far_peers
    for peer in fixed:
        pl.semaphore_signal(barrier, inc=1, device_id=peer, device_id_type=MESH)

    @pl.when(has_left)
    def _():
        pl.semaphore_signal(barrier, inc=1, device_id=at(h, s - 1), device_id_type=MESH)

    @pl.when(has_right)
    def _():
        pl.semaphore_signal(barrier, inc=1, device_id=at(h, s + 1), device_id_type=MESH)

    pl.semaphore_wait(
        barrier, len(fixed) + has_left.astype(jnp.int32) + has_right.astype(jnp.int32)
    )

    width = BAND * LON
    near = own * LON
    left_far, right_far = 2 * width, 0

    def halo(slot, low, source, target, space):
        return pltpu.make_async_remote_copy(
            src_ref=fields.at[low : low + CP, source : source + near],
            dst_ref=ext.at[low : low + CP, target : target + near],
            send_sem=halo_send.at[slot], recv_sem=halo_recv.at[slot],
            device_id=at(h, space), device_id_type=MESH,
        )

    left_near = [halo(0, 0, 0, left_far, s - 1)]
    right_near = [halo(1, 0, near, right_far + near, s + 1)]
    right_more = [halo(2, 0, 0, right_far, s + 1), halo(3, CP, near, right_far + near, s + 1)]
    left_more = [halo(4, 0, near, left_far + near, s - 1), halo(5, CP, 0, left_far, s - 1)]
    lower = h == 0
    upper = jnp.logical_not(lower)
    sends = (
        (has_left, left_near), (has_right, right_near),
        (has_left & upper, left_more), (has_right & lower, right_more),
    )
    arrivals = (
        (has_right, left_near), (has_left, right_near),
        (has_right & upper, left_more), (has_left & lower, right_more),
    )

    def start_all(group):
        def run():
            for copy in group:
                copy.start()
        return run

    def await_sent(group):
        def run():
            for copy in group:
                copy.wait_send()
        return run

    def await_arrived(group):
        def run():
            for copy in group:
                copy.wait_recv()
        return run

    swap = pltpu.make_async_remote_copy(
        src_ref=seeds, dst_ref=all_seeds.at[h],
        send_sem=seed_sem.at[0], recv_sem=seed_sem.at[1],
        device_id=member_peer, device_id_type=MESH,
    )
    swap.start()

    for condition, group in sends:
        pl.when(condition)(start_all(group))

    all_seeds[h] = seeds[...]
    ext[:, width : 2 * width] = fields[...]
    total[...] = jnp.zeros_like(total)

    @pl.when(jnp.logical_not(has_left))
    def _():
        ext[:, 0:width] = jnp.zeros((2 * CP, width), BF16)

    @pl.when(jnp.logical_not(has_right))
    def _():
        ext[:, 2 * width : 3 * width] = jnp.zeros((2 * CP, width), BF16)

    swap.wait()

    n_in = 2 * own + 6
    base_row = s * BAND + h * own - 4
    lon = lax.broadcasted_iota(jnp.int32, (NOISE, LON), 1)
    chan = lax.broadcasted_iota(jnp.int32, (NOISE, LON), 0)
    lane_term = lon * 31 + chan * 104729
    late_term = chan * 97 + lon * 13

    def noise_member(m, carry):
        seed = all_seeds[m // 2, pl.ds(m % 2, 1), :]
        seed7 = jnp.concatenate([seed, seed], axis=1) * 7
        for j in range(10):
            hashed = modulo(jnp.maximum(seed7 + (base_row + j) * 1439 + lane_term, 0), 65521)
            folded = jnp.where(hashed >= 46340, hashed - 46340, hashed)
            mixed = modulo(folded * folded + late_term, 65521)
            value = mixed.astype(F32) / 32760.0 - 1.0
            value = value * aux[8 + j : 9 + j, :]
            value = value.astype(BF16).astype(F32)
            zero = jnp.zeros_like(value)
            for b, shift in enumerate((1, 0, LON - 1)):
                moved = pltpu.roll(value, shift, 1) if shift else value
                xn3[m, b * 16 : b * 16 + 16, j * LON : (j + 1) * LON] = jnp.concatenate(
                    [moved, zero], axis=0
                ).astype(BF16)
        return carry

    lax.fori_loop(0, MEM, noise_member, 0)

    for condition, group in sends:
        pl.when(condition)(await_sent(group))
    for condition, group in arrivals:
        pl.when(condition)(await_arrived(group))

    def ext_cols(j):
        return pl.ds(pl.multiple_of(h * (own * LON), own * LON) + j * LON, LON)

    row_of = lax.broadcasted_iota(jnp.int32, (CP, LON), 0)
    for j in range(10):
        value = ext[0:CP, ext_cols(j)].astype(F32)
        for b, shift in enumerate((1, 0, LON - 1)):
            moved = pltpu.roll(value, shift, 1) if shift else jnp.where(row_of == C, 1.0, value)
            xs3[b * CP : (b + 1) * CP, j * LON : (j + 1) * LON] = moved.astype(BF16)

    def cols(j, n=1):
        return slice(j * LON, (j + n) * LON)

    for k in range(8):
        pre_common[:, cols(k)] = (
            dot(w1s[0], xs3[:, cols(k)])
            + dot(w1s[1], xs3[:, cols(k + 1)])
            + dot(w1s[2], xs3[:, cols(k + 2)])
            + b1[...]
        )

    def forward(m, carry):
        for k in range(8):
            noise9 = jnp.concatenate([xn3[m, :, cols(k + a)] for a in range(3)], axis=0)
            pre = pre_common[:, cols(k)] + dot(w1n[...], noise9)
            sig = 1.0 / (1.0 + jnp.exp(-pre))
            hid = pre * sig * aux[9 + k : 10 + k, :]
            hid = hid.astype(BF16).astype(F32)
            if 2 <= k < 6:
                gate[m, :, cols(k - 2)] = sig * (1.0 + pre * (1.0 - sig)) * aux[9 + k : 10 + k, :]
            for b, shift in enumerate((1, 0, LON - 1)):
                moved = pltpu.roll(hid, shift, 1) if shift else hid
                h3[m, b * HID : (b + 1) * HID, cols(k)] = moved.astype(BF16)
        for n in range(6):
            hid9 = jnp.concatenate([h3[m, :, cols(n + a)] for a in range(3)], axis=0)
            state = ext[0:CP, ext_cols(n + 2)].astype(F32)
            outs[m, :, cols(n)] = (state + b2[...] + dot(w2f[...], hid9)).astype(BF16)
        return carry

    lax.fori_loop(0, MEM, forward, 0)

    for n in range(6):
        values = [outs[m, :, cols(n)].astype(F32) for m in range(MEM)]
        target = ext[CP : 2 * CP, ext_cols(n + 2)].astype(F32)
        sums = [jnp.zeros((CP, LON), F32)] * MEM
        for m in range(MEM):
            for q in range(m + 1, MEM):
                term = slope(values[m] - values[q])
                sums[m] = sums[m] + term
                sums[q] = sums[q] - term
        for m in range(MEM):
            grad = aux[n : n + 1, :] * (
                slope(values[m] - target) * (1.0 / MEM) - sums[m] * (1.0 / (MEM * (MEM - 1)))
            )
            grad = grad.astype(BF16).astype(F32)
            for b, shift in enumerate((LON - 1, 0, 1)):
                moved = pltpu.roll(grad, shift, 1) if shift else grad
                og3[m, b * CP : (b + 1) * CP, cols(n)] = moved.astype(BF16)

    first_row = jnp.where(
        lax.broadcasted_iota(jnp.int32, (8, own * LON), 0) == 0, 1.0, 0.0
    ).astype(BF16)
    per_tap = CP + NOISE
    second = 9 * per_tap
    keep_c = lax.broadcasted_iota(jnp.int32, (CP, HID), 0) < C

    def backward(m, carry):
        for p in range(4):
            hidden_grad = (
                dot(w2t[0], og3[m, :, cols(p + 2)])
                + dot(w2t[1], og3[m, :, cols(p + 1)])
                + dot(w2t[2], og3[m, :, cols(p)])
            )
            grad = (hidden_grad * gate[m, :, cols(p)]).astype(BF16).astype(F32)
            for b, shift in enumerate((LON - 1, 0, 1)):
                moved = pltpu.roll(grad, shift, 1) if shift else grad
                pg3[m, b * HID : (b + 1) * HID, cols(p)] = moved.astype(BF16)
        own_out = og3[m, CP : 2 * CP, cols(2, own)]
        own_pre = pg3[m, HID : 2 * HID, cols(1, own)]
        for a in range(3):
            part = dot_nt(own_out, h3[m, :, cols(2 + a, own)])
            first_s = dot_nt(xs3[:, cols(3 + a, own)], own_pre)
            first_n = dot_nt(xn3[m, :, cols(3 + a, own)], own_pre)
            for b in range(3):
                tap = 3 * a + b
                at_row = second + tap * CP
                total[at_row : at_row + CP, :] += part[:, b * HID : (b + 1) * HID]
                chunk = first_s[b * CP : (b + 1) * CP]
                if tap != 4:
                    chunk = jnp.where(keep_c, chunk, 0.0)
                total[tap * per_tap : tap * per_tap + CP, :] += chunk
                total[tap * per_tap + CP : (tap + 1) * per_tap, :] += first_n[
                    b * 16 : b * 16 + NOISE
                ]
        at_row = second + 9 * CP
        total[at_row : at_row + 8, 0:CP] += dot_nt(first_row, own_out)
        return carry

    lax.fori_loop(0, MEM, backward, 0)

    rows = total.shape[0]
    half, quarter, piece = rows // 2, rows // 8, rows // 32
    keep1 = pl.multiple_of(core * half, half)
    away1 = pl.multiple_of((1 - core) * half, half)
    first_copy = pltpu.make_async_remote_copy(
        src_ref=total.at[pl.ds(away1, half)], dst_ref=recv1,
        send_sem=red_send.at[0], recv_sem=red_recv.at[0],
        device_id=core_peer, device_id_type=MESH,
    )
    first_copy.start()

    for t in range(own):
        value = jnp.zeros((CP, LON), F32)
        for m in range(MEM):
            grad9 = jnp.concatenate([pg3[m, :, cols(t + 2 - a)] for a in range(3)], axis=0)
            value = value + dot(w1t[...], grad9)
            value = value + og3[m, CP : 2 * CP, cols(t + 2)].astype(F32)
        state_out[h, :, cols(t)] = value
    state_copy = pltpu.make_async_remote_copy(
        src_ref=state_out.at[h], dst_ref=state_out.at[h],
        send_sem=state_sem.at[0], recv_sem=state_sem.at[1],
        device_id=member_peer, device_id_type=MESH,
    )

    first_copy.wait()
    total[pl.ds(keep1, half), :] += recv1[...]
    send2[...] = total[pl.ds(keep1, half), :].astype(BF16)
    copies = []
    for d in (1, 2, 3):
        qm = 1 - h if d & 2 else h
        qy = 1 - quad_y if d & 1 else quad_y
        start = pl.multiple_of((qm * 2 + qy) * quarter, quarter)
        copies.append(pltpu.make_async_remote_copy(
            src_ref=send2.at[pl.ds(start, quarter)], dst_ref=recv2.at[d - 1],
            send_sem=red_send.at[d], recv_sem=red_recv.at[d],
            device_id=quad_peers[d - 1], device_id_type=MESH,
        ))
        copies[-1].start()
    state_copy.start()
    for copy in copies:
        copy.wait()
    keep2 = pl.multiple_of(keep1 + quad * quarter, quarter)
    value = total[pl.ds(keep2, quarter), :]
    for d in range(3):
        value = value + recv2[d].astype(F32)
    total[pl.ds(keep2, quarter), :] = value
    send3[...] = value.astype(BF16)
    copies = []
    for d in (1, 2, 3):
        other = flip(zed, d, 1, 4)
        start = pl.multiple_of(other * piece, piece)
        copies.append(pltpu.make_async_remote_copy(
            src_ref=send3.at[pl.ds(start, piece)], dst_ref=recv3.at[d - 1],
            send_sem=red_send.at[3 + d], recv_sem=red_recv.at[3 + d],
            device_id=zed_peers[d - 1], device_id_type=MESH,
        ))
        copies[-1].start()
    for copy in copies:
        copy.wait()
    keep3 = pl.multiple_of(keep2 + zed * piece, piece)
    value = total[pl.ds(keep3, piece), :]
    for d in range(3):
        value = value + recv3[d].astype(F32)
    for k in range(bits):
        part4[k] = value
        copy = pltpu.make_async_remote_copy(
            src_ref=part4.at[k], dst_ref=recv4.at[k],
            send_sem=more_send.at[k], recv_sem=more_recv.at[k],
            device_id=far_peers[k], device_id_type=MESH,
        )
        copy.start()
        copy.wait()
        value = value + recv4[k]
    gathered[pl.ds(keep3, piece), :] = value.astype(BF16)

    slot = 0
    for start, size, peers in (
        (keep3, piece, zed_peers), (keep2, quarter, quad_peers), (keep1, half, [core_peer])
    ):
        copies = []
        for peer in peers:
            copies.append(pltpu.make_async_remote_copy(
                src_ref=gathered.at[pl.ds(start, size)], dst_ref=gathered.at[pl.ds(start, size)],
                send_sem=gat_send.at[slot], recv_sem=gat_recv.at[slot],
                device_id=peer, device_id_type=MESH,
            ))
            copies[-1].start()
            slot += 1
        for copy in copies:
            copy.wait()

    everything = gathered[...].astype(F32)
    squares = jnp.sum(everything * everything)
    count = 9 * HID * (C + NOISE) + HID + 9 * C * HID + C
    norm = jnp.sqrt(jnp.broadcast_to(squares, (8, HID)))
    factor = jnp.minimum(1.0, math.sqrt(count) / norm)
    grads_out[...] = everything * factor[0:1, :]
    state_copy.wait()


def local(
    state_field, target_field, noise_seeds, first_weight, first_bias, second_weight, second_bias
):
    C, band, lon = state_field.shape
    hid = first_weight.shape[1]
    noise = first_weight.shape[2] - C
    space_size = lax.axis_size("space")
    members = noise_seeds.shape[0] * lax.axis_size("member")
    total_rows = band * space_size
    cp = (C + 1 + 15) // 16 * 16
    own = band // 2
    fields = jnp.pad(
        jnp.stack([state_field, target_field]), ((0, 0), (0, cp - C), (0, 0), (0, 0))
    ).reshape(2 * cp, band * lon)
    seeds = jnp.broadcast_to(
        jnp.pad(noise_seeds, (0, 8 - noise_seeds.shape[0]))[:, None], (8, 128)
    )
    base = lax.axis_index("space") * band + lax.axis_index("member") * own
    row_ids = base - 4 + jnp.arange(10, dtype=jnp.int32)
    inside = ((row_ids >= 0) & (row_ids < total_rows)).astype(F32)
    out_ids = row_ids[2:8]
    area = jnp.sin(math.pi * (out_ids.astype(F32) + 0.5) / total_rows) * inside[2:8]
    aux = jnp.concatenate([area, jnp.zeros((2,), F32), inside, jnp.zeros((6,), F32)])
    aux = jnp.broadcast_to(aux[:, None], (24, lon))
    w1_state = jnp.pad(first_weight[:, :, :C], ((0, 0), (0, 0), (0, cp - C)))
    w1_noise = jnp.pad(first_weight[:, :, C:], ((0, 0), (0, 0), (0, 16 - noise)))
    w2 = jnp.pad(second_weight, ((0, 0), (0, cp - C), (0, 0)))
    w1s = w1_state.reshape(3, 3, hid, cp).transpose(0, 2, 1, 3).reshape(3, hid, 3 * cp)
    w1n = w1_noise.transpose(1, 0, 2).reshape(hid, 9 * 16)
    w2f = w2.transpose(1, 0, 2).reshape(cp, 9 * hid)
    w2t = w2.reshape(3, 3, cp, hid).transpose(0, 3, 1, 2).reshape(3, hid, 3 * cp)
    w1t = w1_state.transpose(2, 0, 1).reshape(cp, 9 * hid)
    b1 = first_bias[:, None]
    b2 = jnp.pad(second_bias, (0, cp - C))[:, None]
    per_tap = cp + noise
    used = 9 * per_tap + 9 * cp + 8
    rows = (used + 511) // 512 * 512
    half, quarter, piece = rows // 2, rows // 8, rows // 32
    far = max(1, space_size.bit_length() - 5)
    vmem = pl.BlockSpec(memory_space=pltpu.VMEM)
    dma = pltpu.SemaphoreType.DMA
    cfg = (C, cp, hid, lon, band, members, noise)
    grads, state = pl.pallas_call(
        functools.partial(kernel, space_size, cfg),
        out_shape=(
            jax.ShapeDtypeStruct((rows, hid), F32),
            jax.ShapeDtypeStruct((2, cp, own * lon), F32),
        ),
        in_specs=[vmem] * 10,
        out_specs=(vmem, vmem),
        scratch_shapes=[
            pltpu.VMEM((2 * cp, 3 * band * lon), BF16),
            pltpu.VMEM((2, 8, 128), jnp.int32),
            pltpu.VMEM((3 * cp, 10 * lon), BF16),
            pltpu.VMEM((members, 48, 10 * lon), BF16),
            pltpu.VMEM((hid, 8 * lon), F32),
            pltpu.VMEM((members, 3 * hid, 8 * lon), BF16),
            pltpu.VMEM((members, hid, 4 * lon), F32),
            pltpu.VMEM((members, cp, 6 * lon), BF16),
            pltpu.VMEM((members, 3 * cp, 6 * lon), BF16),
            pltpu.VMEM((members, 3 * hid, 4 * lon), BF16),
            pltpu.VMEM((rows, hid), F32),
            pltpu.VMEM((half, hid), F32),
            pltpu.VMEM((half, hid), BF16),
            pltpu.VMEM((3, quarter, hid), BF16),
            pltpu.VMEM((quarter, hid), BF16),
            pltpu.VMEM((3, piece, hid), BF16),
            pltpu.VMEM((far, piece, hid), F32),
            pltpu.VMEM((far, piece, hid), F32),
            pltpu.VMEM((rows, hid), BF16),
            dma((6,)), dma((6,)), dma((2,)), dma((2,)),
            dma((7,)), dma((7,)), dma((7,)), dma((7,)), dma((far,)), dma((far,)),
        ],
        compiler_params=pltpu.CompilerParams(
            collective_id=0, has_side_effects=True, vmem_limit_bytes=48 * 1024 * 1024
        ),
    )(fields, seeds, aux, w1s, w1n, b1, w2f, b2, w2t, w1t)
    state_gradient = state.reshape(2, cp, own, lon)[:, :C].transpose(1, 0, 2, 3).reshape(
        C, band, lon
    )
    first = grads[: 9 * per_tap].reshape(9, per_tap, hid)
    first_w = jnp.concatenate([first[:, :C], first[:, cp:]], axis=1).transpose(0, 2, 1)
    first_b = first[4, C]
    second = grads[9 * per_tap : 9 * per_tap + 9 * cp].reshape(9, cp, hid)[:, :C]
    second_b = grads[9 * per_tap + 9 * cp, :C]
    return state_gradient, first_w, first_b, second, second_b


def solution(mesh):
    placed = (P(None, "space", None), P(None, "space", None), P("member"), P(), P(), P(), P())
    return jax.shard_map(
        local,
        mesh=mesh,
        in_specs=placed,
        out_specs=(P(None, "space", None), P(), P(), P(), P()),
        check_vma=False,
    )
```

```python
import functools
import math

import jax
import jax.numpy as jnp
from jax import lax
from jax.experimental import pallas as pl
from jax.experimental.pallas import tpu as pltpu
from jax.sharding import PartitionSpec as P

SMOOTH_SQ = 0.01
MESH = pl.DeviceIdType.MESH
F32 = jnp.float32
BF16 = jnp.bfloat16
NT = (((1,), (1,)), ((), ()))


def modulo(value, divisor):
    quotient = (value.astype(F32) * (1.0 / divisor)).astype(jnp.int32)
    left = value - quotient * divisor
    left = jnp.where(left < 0, left + divisor, left)
    return jnp.where(left >= divisor, left - divisor, left)


def slope(diff):
    return diff * lax.rsqrt(diff * diff + SMOOTH_SQ)


def dot(a, b):
    return jnp.dot(a, b, preferred_element_type=F32)


def dot_nt(a, b):
    return lax.dot_general(a, b, NT, preferred_element_type=F32)


def kernel(
    space_size, cfg,
    fields, seeds, aux, w1s, w1n, b1, w2f, b2, w2t, w1t,
    grads_out, state_out,
    ext, all_seeds, xs3, xn3, pre_common, h3, gate, outs, og3, pg3, total, recv1, send2, recv2, send3, recv3, recv4, part4,
    gathered,
    halo_send, halo_recv, seed_sem, state_sem, red_send, red_recv, gat_send, gat_recv, more_send, more_recv,
):
    C, CP, HID, LON, BAND, MEM, NOISE = cfg
    own = BAND // 2
    s = lax.axis_index("space")
    h = lax.axis_index("member")
    has_left = s > 0
    has_right = s < space_size - 1
    bits = (space_size.bit_length() - 1) - 4
    core = s % 2
    quad = h * 2 + (s // 2) % 2
    quad_y = (s // 2) % 2
    zed = (s // 4) % 4

    def flip(value, mask, unit, width):
        digit = (value // unit) % width
        flipped = jnp.int32(0)
        place = 1
        while place < width:
            bit = (digit // place) % 2
            if mask & place:
                bit = 1 - bit
            flipped = flipped + bit * place
            place *= 2
        return value + (flipped - digit) * unit

    def at(member, space):
        return (member, space)

    core_peer = at(h, flip(s, 1, 1, 2))
    member_peer = at(1 - h, s)
    quad_peers = []
    for d in (1, 2, 3):
        quad_peers.append(at(1 - h if d & 2 else h, flip(s, 1, 2, 2) if d & 1 else s))
    zed_peers = [at(h, flip(s, d, 4, 4)) for d in (1, 2, 3)]
    far_peers = [at(h, flip(s, 1, 16 << k, 2)) for k in range(bits)]

    barrier = pltpu.get_barrier_semaphore()
    fixed = [core_peer, member_peer] + quad_peers + zed_peers + far_peers
    for peer in fixed:
        pl.semaphore_signal(barrier, inc=1, device_id=peer, device_id_type=MESH)

    @pl.when(has_left)
    def _():
        pl.semaphore_signal(barrier, inc=1, device_id=at(h, s - 1), device_id_type=MESH)

    @pl.when(has_right)
    def _():
        pl.semaphore_signal(barrier, inc=1, device_id=at(h, s + 1), device_id_type=MESH)

    pl.semaphore_wait(
        barrier, len(fixed) + has_left.astype(jnp.int32) + has_right.astype(jnp.int32)
    )

    width = BAND * LON
    near = own * LON
    left_far, right_far = 2 * width, 0

    def halo(slot, low, source, target, space):
        return pltpu.make_async_remote_copy(
            src_ref=fields.at[low : low + CP, source : source + near],
            dst_ref=ext.at[low : low + CP, target : target + near],
            send_sem=halo_send.at[slot], recv_sem=halo_recv.at[slot],
            device_id=at(h, space), device_id_type=MESH,
        )

    left_near = [halo(0, 0, 0, left_far, s - 1)]
    right_near = [halo(1, 0, near, right_far + near, s + 1)]
    right_more = [halo(2, 0, 0, right_far, s + 1), halo(3, CP, near, right_far + near, s + 1)]
    left_more = [halo(4, 0, near, left_far + near, s - 1), halo(5, CP, 0, left_far, s - 1)]
    lower = h == 0
    upper = jnp.logical_not(lower)
    sends = (
        (has_left, left_near), (has_right, right_near),
        (has_left & upper, left_more), (has_right & lower, right_more),
    )
    arrivals = (
        (has_right, left_near), (has_left, right_near),
        (has_right & upper, left_more), (has_left & lower, right_more),
    )

    def start_all(group):
        def run():
            for copy in group:
                copy.start()
        return run

    def await_sent(group):
        def run():
            for copy in group:
                copy.wait_send()
        return run

    def await_arrived(group):
        def run():
            for copy in group:
                copy.wait_recv()
        return run

    swap = pltpu.make_async_remote_copy(
        src_ref=seeds, dst_ref=all_seeds.at[h],
        send_sem=seed_sem.at[0], recv_sem=seed_sem.at[1],
        device_id=member_peer, device_id_type=MESH,
    )
    swap.start()

    for condition, group in sends:
        pl.when(condition)(start_all(group))

    all_seeds[h] = seeds[...]
    ext[:, width : 2 * width] = fields[...]
    total[...] = jnp.zeros_like(total)

    @pl.when(jnp.logical_not(has_left))
    def _():
        ext[:, 0:width] = jnp.zeros((2 * CP, width), BF16)

    @pl.when(jnp.logical_not(has_right))
    def _():
        ext[:, 2 * width : 3 * width] = jnp.zeros((2 * CP, width), BF16)

    swap.wait()

    n_in = 2 * own + 6
    base_row = s * BAND + h * own - 4
    lon = lax.broadcasted_iota(jnp.int32, (NOISE, LON), 1)
    chan = lax.broadcasted_iota(jnp.int32, (NOISE, LON), 0)
    lane_term = lon * 31 + chan * 104729
    late_term = chan * 97 + lon * 13

    def noise_member(m, carry):
        seed = all_seeds[m // 2, pl.ds(m % 2, 1), :]
        seed7 = jnp.concatenate([seed, seed], axis=1) * 7
        for j in range(10):
            hashed = modulo(jnp.maximum(seed7 + (base_row + j) * 1439 + lane_term, 0), 65521)
            folded = jnp.where(hashed >= 46340, hashed - 46340, hashed)
            mixed = modulo(folded * folded + late_term, 65521)
            value = mixed.astype(F32) / 32760.0 - 1.0
            value = value * aux[8 + j : 9 + j, :]
            value = value.astype(BF16).astype(F32)
            zero = jnp.zeros_like(value)
            for b, shift in enumerate((1, 0, LON - 1)):
                moved = pltpu.roll(value, shift, 1) if shift else value
                xn3[m, b * 16 : b * 16 + 16, j * LON : (j + 1) * LON] = jnp.concatenate(
                    [moved, zero], axis=0
                ).astype(BF16)
        return carry

    lax.fori_loop(0, MEM, noise_member, 0)

    for condition, group in sends:
        pl.when(condition)(await_sent(group))
    for condition, group in arrivals:
        pl.when(condition)(await_arrived(group))

    def ext_cols(j):
        return pl.ds(pl.multiple_of(h * (own * LON), own * LON) + j * LON, LON)

    row_of = lax.broadcasted_iota(jnp.int32, (CP, LON), 0)
    for j in range(10):
        value = ext[0:CP, ext_cols(j)].astype(F32)
        for b, shift in enumerate((1, 0, LON - 1)):
            moved = pltpu.roll(value, shift, 1) if shift else jnp.where(row_of == C, 1.0, value)
            xs3[b * CP : (b + 1) * CP, j * LON : (j + 1) * LON] = moved.astype(BF16)

    def cols(j, n=1):
        return slice(j * LON, (j + n) * LON)

    for k in range(8):
        pre_common[:, cols(k)] = (
            dot(w1s[0], xs3[:, cols(k)])
            + dot(w1s[1], xs3[:, cols(k + 1)])
            + dot(w1s[2], xs3[:, cols(k + 2)])
            + b1[...]
        )

    def forward(m, carry):
        for k in range(8):
            noise9 = jnp.concatenate([xn3[m, :, cols(k + a)] for a in range(3)], axis=0)
            pre = pre_common[:, cols(k)] + dot(w1n[...], noise9)
            sig = 1.0 / (1.0 + jnp.exp(-pre))
            hid = pre * sig * aux[9 + k : 10 + k, :]
            hid = hid.astype(BF16).astype(F32)
            if 2 <= k < 6:
                gate[m, :, cols(k - 2)] = sig * (1.0 + pre * (1.0 - sig)) * aux[9 + k : 10 + k, :]
            for b, shift in enumerate((1, 0, LON - 1)):
                moved = pltpu.roll(hid, shift, 1) if shift else hid
                h3[m, b * HID : (b + 1) * HID, cols(k)] = moved.astype(BF16)
        for n in range(6):
            hid9 = jnp.concatenate([h3[m, :, cols(n + a)] for a in range(3)], axis=0)
            state = ext[0:CP, ext_cols(n + 2)].astype(F32)
            outs[m, :, cols(n)] = (state + b2[...] + dot(w2f[...], hid9)).astype(BF16)
        return carry

    lax.fori_loop(0, MEM, forward, 0)

    for n in range(6):
        values = [outs[m, :, cols(n)].astype(F32) for m in range(MEM)]
        target = ext[CP : 2 * CP, ext_cols(n + 2)].astype(F32)
        sums = [jnp.zeros((CP, LON), F32)] * MEM
        for m in range(MEM):
            for q in range(m + 1, MEM):
                term = slope(values[m] - values[q])
                sums[m] = sums[m] + term
                sums[q] = sums[q] - term
        for m in range(MEM):
            grad = aux[n : n + 1, :] * (
                slope(values[m] - target) * (1.0 / MEM) - sums[m] * (1.0 / (MEM * (MEM - 1)))
            )
            grad = grad.astype(BF16).astype(F32)
            for b, shift in enumerate((LON - 1, 0, 1)):
                moved = pltpu.roll(grad, shift, 1) if shift else grad
                og3[m, b * CP : (b + 1) * CP, cols(n)] = moved.astype(BF16)

    first_row = jnp.where(
        lax.broadcasted_iota(jnp.int32, (8, own * LON), 0) == 0, 1.0, 0.0
    ).astype(BF16)
    per_tap = CP + NOISE
    second = 9 * per_tap
    keep_c = lax.broadcasted_iota(jnp.int32, (CP, HID), 0) < C

    def backward(m, carry):
        for p in range(4):
            hidden_grad = (
                dot(w2t[0], og3[m, :, cols(p + 2)])
                + dot(w2t[1], og3[m, :, cols(p + 1)])
                + dot(w2t[2], og3[m, :, cols(p)])
            )
            grad = (hidden_grad * gate[m, :, cols(p)]).astype(BF16).astype(F32)
            for b, shift in enumerate((LON - 1, 0, 1)):
                moved = pltpu.roll(grad, shift, 1) if shift else grad
                pg3[m, b * HID : (b + 1) * HID, cols(p)] = moved.astype(BF16)
        own_out = og3[m, CP : 2 * CP, cols(2, own)]
        own_pre = pg3[m, HID : 2 * HID, cols(1, own)]
        for a in range(3):
            part = dot_nt(own_out, h3[m, :, cols(2 + a, own)])
            first_s = dot_nt(xs3[:, cols(3 + a, own)], own_pre)
            first_n = dot_nt(xn3[m, :, cols(3 + a, own)], own_pre)
            for b in range(3):
                tap = 3 * a + b
                at_row = second + tap * CP
                total[at_row : at_row + CP, :] += part[:, b * HID : (b + 1) * HID]
                chunk = first_s[b * CP : (b + 1) * CP]
                if tap != 4:
                    chunk = jnp.where(keep_c, chunk, 0.0)
                total[tap * per_tap : tap * per_tap + CP, :] += chunk
                total[tap * per_tap + CP : (tap + 1) * per_tap, :] += first_n[
                    b * 16 : b * 16 + NOISE
                ]
        at_row = second + 9 * CP
        total[at_row : at_row + 8, 0:CP] += dot_nt(first_row, own_out)
        return carry

    lax.fori_loop(0, MEM, backward, 0)

    rows = total.shape[0]
    half, quarter, piece = rows // 2, rows // 8, rows // 32
    keep1 = pl.multiple_of(core * half, half)
    away1 = pl.multiple_of((1 - core) * half, half)
    first_copy = pltpu.make_async_remote_copy(
        src_ref=total.at[pl.ds(away1, half)], dst_ref=recv1,
        send_sem=red_send.at[0], recv_sem=red_recv.at[0],
        device_id=core_peer, device_id_type=MESH,
    )
    first_copy.start()

    for t in range(own):
        value = jnp.zeros((CP, LON), F32)
        for m in range(MEM):
            grad9 = jnp.concatenate([pg3[m, :, cols(t + 2 - a)] for a in range(3)], axis=0)
            value = value + dot(w1t[...], grad9)
            value = value + og3[m, CP : 2 * CP, cols(t + 2)].astype(F32)
        state_out[h, :, cols(t)] = value
    state_copy = pltpu.make_async_remote_copy(
        src_ref=state_out.at[h], dst_ref=state_out.at[h],
        send_sem=state_sem.at[0], recv_sem=state_sem.at[1],
        device_id=member_peer, device_id_type=MESH,
    )

    first_copy.wait()
    total[pl.ds(keep1, half), :] += recv1[...]
    send2[...] = total[pl.ds(keep1, half), :].astype(BF16)
    copies = []
    for d in (1, 2, 3):
        qm = 1 - h if d & 2 else h
        qy = 1 - quad_y if d & 1 else quad_y
        start = pl.multiple_of((qm * 2 + qy) * quarter, quarter)
        copies.append(pltpu.make_async_remote_copy(
            src_ref=send2.at[pl.ds(start, quarter)], dst_ref=recv2.at[d - 1],
            send_sem=red_send.at[d], recv_sem=red_recv.at[d],
            device_id=quad_peers[d - 1], device_id_type=MESH,
        ))
        copies[-1].start()
    for copy in copies:
        copy.wait()
    state_copy.start()
    keep2 = pl.multiple_of(keep1 + quad * quarter, quarter)
    value = total[pl.ds(keep2, quarter), :]
    for d in range(3):
        value = value + recv2[d].astype(F32)
    total[pl.ds(keep2, quarter), :] = value
    send3[...] = value.astype(BF16)
    copies = []
    for d in (1, 2, 3):
        other = flip(zed, d, 1, 4)
        start = pl.multiple_of(other * piece, piece)
        copies.append(pltpu.make_async_remote_copy(
            src_ref=send3.at[pl.ds(start, piece)], dst_ref=recv3.at[d - 1],
            send_sem=red_send.at[3 + d], recv_sem=red_recv.at[3 + d],
            device_id=zed_peers[d - 1], device_id_type=MESH,
        ))
        copies[-1].start()
    for copy in copies:
        copy.wait()
    keep3 = pl.multiple_of(keep2 + zed * piece, piece)
    value = total[pl.ds(keep3, piece), :]
    for d in range(3):
        value = value + recv3[d].astype(F32)
    for k in range(bits):
        part4[k] = value
        copy = pltpu.make_async_remote_copy(
            src_ref=part4.at[k], dst_ref=recv4.at[k],
            send_sem=more_send.at[k], recv_sem=more_recv.at[k],
            device_id=far_peers[k], device_id_type=MESH,
        )
        copy.start()
        copy.wait()
        value = value + recv4[k]
    gathered[pl.ds(keep3, piece), :] = value.astype(BF16)

    slot = 0
    for start, size, peers in (
        (keep3, piece, zed_peers), (keep2, quarter, quad_peers), (keep1, half, [core_peer])
    ):
        copies = []
        for peer in peers:
            copies.append(pltpu.make_async_remote_copy(
                src_ref=gathered.at[pl.ds(start, size)], dst_ref=gathered.at[pl.ds(start, size)],
                send_sem=gat_send.at[slot], recv_sem=gat_recv.at[slot],
                device_id=peer, device_id_type=MESH,
            ))
            copies[-1].start()
            slot += 1
        for copy in copies:
            copy.wait()

    everything = gathered[...].astype(F32)
    squares = jnp.sum(everything * everything)
    count = 9 * HID * (C + NOISE) + HID + 9 * C * HID + C
    norm = jnp.sqrt(jnp.broadcast_to(squares, (8, HID)))
    factor = jnp.minimum(1.0, math.sqrt(count) / norm)
    grads_out[...] = everything * factor[0:1, :]
    state_copy.wait()


def local(
    state_field, target_field, noise_seeds, first_weight, first_bias, second_weight, second_bias
):
    C, band, lon = state_field.shape
    hid = first_weight.shape[1]
    noise = first_weight.shape[2] - C
    space_size = lax.axis_size("space")
    members = noise_seeds.shape[0] * lax.axis_size("member")
    total_rows = band * space_size
    cp = (C + 1 + 15) // 16 * 16
    own = band // 2
    fields = jnp.pad(
        jnp.stack([state_field, target_field]), ((0, 0), (0, cp - C), (0, 0), (0, 0))
    ).reshape(2 * cp, band * lon)
    seeds = jnp.broadcast_to(
        jnp.pad(noise_seeds, (0, 8 - noise_seeds.shape[0]))[:, None], (8, 128)
    )
    base = lax.axis_index("space") * band + lax.axis_index("member") * own
    row_ids = base - 4 + jnp.arange(10, dtype=jnp.int32)
    inside = ((row_ids >= 0) & (row_ids < total_rows)).astype(F32)
    out_ids = row_ids[2:8]
    area = jnp.sin(math.pi * (out_ids.astype(F32) + 0.5) / total_rows) * inside[2:8]
    aux = jnp.concatenate([area, jnp.zeros((2,), F32), inside, jnp.zeros((6,), F32)])
    aux = jnp.broadcast_to(aux[:, None], (24, lon))
    w1_state = jnp.pad(first_weight[:, :, :C], ((0, 0), (0, 0), (0, cp - C)))
    w1_noise = jnp.pad(first_weight[:, :, C:], ((0, 0), (0, 0), (0, 16 - noise)))
    w2 = jnp.pad(second_weight, ((0, 0), (0, cp - C), (0, 0)))
    w1s = w1_state.reshape(3, 3, hid, cp).transpose(0, 2, 1, 3).reshape(3, hid, 3 * cp)
    w1n = w1_noise.transpose(1, 0, 2).reshape(hid, 9 * 16)
    w2f = w2.transpose(1, 0, 2).reshape(cp, 9 * hid)
    w2t = w2.reshape(3, 3, cp, hid).transpose(0, 3, 1, 2).reshape(3, hid, 3 * cp)
    w1t = w1_state.transpose(2, 0, 1).reshape(cp, 9 * hid)
    b1 = first_bias[:, None]
    b2 = jnp.pad(second_bias, (0, cp - C))[:, None]
    per_tap = cp + noise
    used = 9 * per_tap + 9 * cp + 8
    rows = (used + 511) // 512 * 512
    half, quarter, piece = rows // 2, rows // 8, rows // 32
    far = max(1, space_size.bit_length() - 5)
    vmem = pl.BlockSpec(memory_space=pltpu.VMEM)
    dma = pltpu.SemaphoreType.DMA
    cfg = (C, cp, hid, lon, band, members, noise)
    grads, state = pl.pallas_call(
        functools.partial(kernel, space_size, cfg),
        out_shape=(
            jax.ShapeDtypeStruct((rows, hid), F32),
            jax.ShapeDtypeStruct((2, cp, own * lon), F32),
        ),
        in_specs=[vmem] * 10,
        out_specs=(vmem, vmem),
        scratch_shapes=[
            pltpu.VMEM((2 * cp, 3 * band * lon), BF16),
            pltpu.VMEM((2, 8, 128), jnp.int32),
            pltpu.VMEM((3 * cp, 10 * lon), BF16),
            pltpu.VMEM((members, 48, 10 * lon), BF16),
            pltpu.VMEM((hid, 8 * lon), F32),
            pltpu.VMEM((members, 3 * hid, 8 * lon), BF16),
            pltpu.VMEM((members, hid, 4 * lon), F32),
            pltpu.VMEM((members, cp, 6 * lon), BF16),
            pltpu.VMEM((members, 3 * cp, 6 * lon), BF16),
            pltpu.VMEM((members, 3 * hid, 4 * lon), BF16),
            pltpu.VMEM((rows, hid), F32),
            pltpu.VMEM((half, hid), F32),
            pltpu.VMEM((half, hid), BF16),
            pltpu.VMEM((3, quarter, hid), BF16),
            pltpu.VMEM((quarter, hid), BF16),
            pltpu.VMEM((3, piece, hid), BF16),
            pltpu.VMEM((far, piece, hid), F32),
            pltpu.VMEM((far, piece, hid), F32),
            pltpu.VMEM((rows, hid), BF16),
            dma((6,)), dma((6,)), dma((2,)), dma((2,)),
            dma((7,)), dma((7,)), dma((7,)), dma((7,)), dma((far,)), dma((far,)),
        ],
        compiler_params=pltpu.CompilerParams(
            collective_id=0, has_side_effects=True, vmem_limit_bytes=48 * 1024 * 1024
        ),
    )(fields, seeds, aux, w1s, w1n, b1, w2f, b2, w2t, w1t)
    state_gradient = state.reshape(2, cp, own, lon)[:, :C].transpose(1, 0, 2, 3).reshape(
        C, band, lon
    )
    first = grads[: 9 * per_tap].reshape(9, per_tap, hid)
    first_w = jnp.concatenate([first[:, :C], first[:, cp:]], axis=1).transpose(0, 2, 1)
    first_b = first[4, C]
    second = grads[9 * per_tap : 9 * per_tap + 9 * cp].reshape(9, cp, hid)[:, :C]
    second_b = grads[9 * per_tap + 9 * cp, :C]
    return state_gradient, first_w, first_b, second, second_b


def solution(mesh):
    placed = (P(None, "space", None), P(None, "space", None), P("member"), P(), P(), P(), P())
    return jax.shard_map(
        local,
        mesh=mesh,
        in_specs=placed,
        out_specs=(P(None, "space", None), P(), P(), P(), P()),
        check_vma=False,
    )
```
